32 devices in a mesh: row: 4 (over y, x), col: 8 (over z, core).
Axes of the slice: x: 2, y: 2, z: 4, core: 2. Of those that a mesh axis runs over, the one named last changes fastest.
Arguments:
- root_inverse: bfloat16 [4096, 4096], P('row', 'col'), may hold values from -16 to 16
- factor: bfloat16 [4096, 4, 4096], P('row', None, 'col'), may hold values from -0.59765625 to 0.59765625
- inverse_diag: bfloat16 [4096, 4, 4096], P('row', None, 'col'), may hold values from -6 to 6
- structure: int32 [4, 32], replicated, may hold values 0 or 1
Outputs:
- ainv_rk: bfloat16 [4096, 4, 4096], P('row', None, 'col')
- ainv_kk: bfloat16 [4096, 4, 4096], P('row', None, 'col')
The draws below stay inside these ranges and needn't reach their ends.
All inputs are finite; a program needn't handle non-finite values.
Results may differ from the reference program's by a relative error of at most 0.014.
Values may be sent and summed in bfloat16 or wider, within the bound.
A program may use at most 128 MiB of HBM per device.

```python
import math
import jax
import jax.numpy as jnp
from jax import lax

W = 4096
BLK = 128
NKID = 4
NBLK = 32
N_ROW = 4


def draw_root_inverse(key, part):
    noise_draw = jax.random.normal(key, (W, W), jnp.float32)
    symmetric = (noise_draw + noise_draw.T) * (0.7071 / math.sqrt(W))
    matrix = symmetric + 1.5 * jnp.eye(W, dtype=jnp.float32)
    return matrix.astype(jnp.bfloat16)


def place_ends(result, key, least, top_value):
    dims = result.shape
    place = [jax.random.randint(jax.random.fold_in(key, axis), (), 0, dims[axis]) for axis in range(len(dims))]
    result = result.at[tuple(place)].set(least)
    longest = dims.index(max(dims))
    place[longest] = (place[longest] + 1) % dims[longest]
    return result.at[tuple(place)].set(top_value)


def block_levels(rng, dims, split, least, largest):
    level = 1.0
    for axis_at, blocks in split:
        draws = jax.random.uniform(jax.random.fold_in(jax.random.fold_in(rng, 6), axis_at), (blocks,), jnp.float32, least / len(split), largest / len(split))
        level = level * jnp.repeat(jnp.exp(draws), dims[axis_at] // blocks).reshape((-1,) + (1,) * (len(dims) - 1 - axis_at))
    return level


def noise(key, dims, deviation, bound, shards=(), held_as=jnp.bfloat16):
    level = block_levels(key, dims, shards, -0.22, 0.18) if shards else 1.0
    entries = jax.random.normal(key, dims, jnp.float32) * deviation * level
    return jnp.minimum(jnp.maximum(entries, -bound), bound).astype(held_as)


def setup_inputs(seed: int = 0) -> dict:
    key_of = jax.random.split(jax.random.key(seed), 5)
    return {
        "root_inverse": draw_root_inverse(jax.random.fold_in(key_of[4], 71), 0),
        "factor": noise(key_of[1], (W, NKID, W), 0.1, 0.59765625, ((0, 4), (2, 8))),
        "inverse_diag": noise(key_of[2], (W, NKID, W), 1.0, 6.0, ((0, 4), (2, 8))),
        "structure": place_ends((jax.random.randint(key_of[3], (NKID, NBLK), 0, 4) < 3).astype(jnp.int32), jax.random.fold_in(key_of[3], 1), 0, 1),
    }


def reference(root_inverse, factor, inverse_diag, structure):
    row_mask = jnp.repeat(structure, BLK, axis=1).T.astype(factor.dtype)
    masked = factor * row_mask[:, :, None]
    product = jnp.einsum('ik,knj->inj', root_inverse.astype(jnp.float32), masked.astype(jnp.float32), precision=lax.Precision.HIGHEST)
    ainv_rk = (-product).astype(jnp.bfloat16)
    group_rows = W // N_ROW
    masked_wide = masked.astype(jnp.float32)
    inverse_wide = ainv_rk.astype(jnp.float32)

    def add_group(group, running):
        offset = (group * group_rows).astype(jnp.int32)
        left_part = lax.dynamic_slice_in_dim(masked_wide, offset, group_rows, 0)
        right_part = lax.dynamic_slice_in_dim(inverse_wide, offset, group_rows, 0)
        term = jnp.einsum('kni,knj->inj', left_part, right_part, precision=lax.Precision.HIGHEST)
        return running + term.astype(jnp.bfloat16).astype(jnp.float32)

    running = jnp.zeros(inverse_diag.shape, jnp.float32)
    running = lax.fori_loop(0, N_ROW, add_group, running)
    ainv_kk = (inverse_diag.astype(jnp.float32) - running).astype(jnp.bfloat16)
    return ainv_rk, ainv_kk
```

```python
import functools

import jax
import jax.numpy as jnp
from jax import lax
from jax.experimental import pallas as pl
from jax.experimental.pallas import tpu as pltpu
from jax.sharding import PartitionSpec as P

BLK = 128
CORES = 2
MESH = pl.DeviceIdType.MESH


def kernel(
    n_row, n_col, root_in, m_in, p_out, t_out, m_line, m_plane,
    root, col_buf, chunk_buf, p_buf, pt_buf, part_buf, sum_buf, t_buf,
    own_sem, up_send, up_recv, down_send, down_recv, mate_send, mate_recv,
    plane_send, plane_recv, part_send, part_recv, load_sem, out_sem, t_sem,
):
    kids, rows, cols = m_in.shape
    n_z = n_col // CORES
    per_row = rows // cols
    r, c = lax.axis_index("row"), lax.axis_index("col")
    z, core = c // CORES, c % CORES
    mate = z * CORES + 1 - core

    barrier = pltpu.get_barrier_semaphore()

    def greet(dev):
        pl.semaphore_signal(barrier, inc=1, device_id=dev, device_id_type=MESH)

    greet((r, mate))
    for d in range(1, n_row):
        greet((lax.rem(r + d, n_row), c))

    for step in (1, n_z - 1):
        greet((r, lax.rem(z + step, n_z) * CORES + core))

    own = [
        pltpu.make_async_copy(root_in, root.at[c], own_sem.at[0]),
        pltpu.make_async_copy(m_in, m_line.at[:, c], own_sem.at[1]),
        pltpu.make_async_copy(m_in, m_plane.at[:, r], own_sem.at[2]),
    ]
    for copy in own:
        copy.start()
    for copy in own:
        copy.wait()

    pl.semaphore_wait(barrier, n_row + 2)

    def slot(item, at):
        return root.at[at] if isinstance(item, int) else m_line.at[item - 1, at]

    def up(item, h, at):
        ref = slot(item, at)
        return pltpu.make_async_remote_copy(
            ref, ref, up_send.at[item, h], up_recv.at[item, h], (r, c + CORES), MESH)

    def down(item, h, at):
        ref = slot(item, at)
        return pltpu.make_async_remote_copy(
            ref, ref, down_send.at[item, h], down_recv.at[item, h], (r, c - CORES), MESH)

    def share(item, zz, at):
        ref = slot(item, at)
        return pltpu.make_async_remote_copy(
            ref, ref, mate_send.at[item, zz], mate_recv.at[item, zz], (r, mate), MESH)

    def begin(item):
        @pl.when(z < n_z - 1)
        def _():
            up(item, 0, c).start()

        @pl.when(z > 0)
        def _():
            down(item, 0, c).start()

        share(item, z, c).start()

    def arrive(item, h):
        low, high = z - 1 - h, z + 1 + h

        @pl.when(low >= 0)
        def _():
            at = low * CORES + core
            up(item, h, at).wait_recv()

            @pl.when((z < n_z - 1) & (h < n_z - 2))
            def _():
                up(item, h + 1, at).start()

            share(item, low, at).start()

        @pl.when(high < n_z)
        def _():
            at = high * CORES + core
            down(item, h, at).wait_recv()

            @pl.when((z > 0) & (h < n_z - 2))
            def _():
                down(item, h + 1, at).start()

            share(item, high, at).start()

    def finish_line(item):
        def hop(h, _):
            @pl.when((z < n_z - 1) & (z - h >= 0))
            def _():
                up(item, h, c - h * CORES).wait_send()

            @pl.when((z > 0) & (z + h < n_z))
            def _():
                down(item, h, c + h * CORES).wait_send()

            return 0

        lax.fori_loop(0, n_z - 1, hop, 0)

        def mates(zz, _):
            share(item, zz, zz * CORES + core).wait_send()
            return 0

        lax.fori_loop(0, n_z, mates, 0)

    def to_row(n, d):
        ref = m_plane.at[n, r]
        return pltpu.make_async_remote_copy(
            ref, ref, plane_send.at[n, d - 1], plane_recv.at[n, d - 1],
            (lax.rem(r + d, n_row), c), MESH)

    def from_row(n, d):
        ref = m_plane.at[n, lax.rem(r - d + n_row, n_row)]
        return pltpu.make_async_remote_copy(
            ref, ref, plane_send.at[n, d - 1], plane_recv.at[n, d - 1],
            (lax.rem(r + d, n_row), c), MESH)

    def send_plane(n):
        for d in range(1, n_row):
            to_row(n, d).start()

    def part_copy(n, at):
        half = lax.rem(at, per_row)
        return pltpu.make_async_remote_copy(
            part_buf.at[n, at], sum_buf.at[n, r, half], part_send.at[n, at],
            part_recv.at[n, r, half], (at // per_row, c), MESH)

    def p_store(n):
        return pltpu.make_async_copy(p_buf, p_out.at[n], out_sem)

    def make_p(n):
        for d in range(1, n_row):
            from_row(n, d).wait_recv()
        load = pltpu.make_async_copy(m_plane.at[n], col_buf, load_sem.at[0])
        load.start()

        @pl.when(n > 0)
        def _():
            p_store(n - 1).wait()

        load.wait()
        tile = min(256, rows)

        def one(t, _):
            at = pl.ds(pl.multiple_of(t * tile, tile), tile)
            total = jnp.zeros((tile, cols), jnp.float32)
            for k in range(n_col):
                block = col_buf[k // per_row, pl.ds((k % per_row) * cols, cols), :]
                total += jnp.dot(root[k, at, :], block, preferred_element_type=jnp.float32)
            total = -total
            p_buf[at, :] = total.astype(p_buf.dtype)
            pt_buf[t, :, :] = total.T.astype(pt_buf.dtype)
            return 0

        lax.fori_loop(0, rows // tile, one, 0)
        p_store(n).start()

    def chunk_load(n, zz, i):
        return pltpu.make_async_copy(
            m_line.at[n, zz * CORES + i], chunk_buf.at[i], load_sem.at[1 + i])

    def consume(n, zz):
        for i in range(CORES):
            chunk_load(n, zz, i).start()
        tile = min(256, rows)
        for i in range(CORES):
            chunk_load(n, zz, i).wait()
            at = zz * CORES + i
            part = jnp.zeros((cols, cols), jnp.float32)
            for t in range(rows // tile):
                part += jnp.dot(
                    pt_buf[t, :, :], chunk_buf[i, pl.ds(t * tile, tile), :],
                    preferred_element_type=jnp.float32)
            part = part.astype(part_buf.dtype)
            owner = at // per_row

            @pl.when(owner == r)
            def _():
                sum_buf[n, r, lax.rem(at, per_row)] = part

            @pl.when(owner != r)
            def _():
                part_buf[n, at] = part
                part_copy(n, at).start()

    def t_store(n):
        return pltpu.make_async_copy(t_buf, t_out.at[n], t_sem)

    def finish_sum(n):
        @pl.when(n > 0)
        def _():
            t_store(n - 1).wait()

        for half in range(per_row):
            total = jnp.zeros((cols, cols), jnp.float32)
            for d in range(1, n_row):
                src = lax.rem(r + d, n_row)
                ref = sum_buf.at[n, src, half]
                pltpu.make_async_remote_copy(
                    ref, ref, part_send.at[n, 0], part_recv.at[n, src, half],
                    (src, c), MESH).wait_recv()
            for src in range(n_row):
                total += sum_buf[n, src, half].astype(jnp.float32)
            t_buf[pl.ds(half * cols, cols), :] = total.T.astype(t_buf.dtype)
        t_store(n).start()

    def wait_mate(item, zz):
        share(item, zz, zz * CORES + 1 - core).wait_recv()

    begin(0)
    send_plane(0)
    send_plane(1)

    def root_hop(h, _):
        arrive(0, h)
        return 0

    lax.fori_loop(0, n_z - 1, root_hop, 0)

    def root_mates(zz, _):
        wait_mate(0, zz)
        return 0

    def kid(n, _):
        item = n + 1

        @pl.when(n < kids - 2)
        def _():
            send_plane(n + 2)

        make_p(n)
        wait_mate(item, z)
        consume(n, z)

        def hop(h, _):
            arrive(item, h)

            @pl.when((h == n_z - 2) & (n < kids - 1))
            def _():
                begin(item + 1)

            low, high = z - 1 - h, z + 1 + h

            @pl.when(low >= 0)
            def _():
                wait_mate(item, low)
                consume(n, low)

            @pl.when(high < n_z)
            def _():
                wait_mate(item, high)
                consume(n, high)

            return 0

        lax.fori_loop(0, n_z - 1, hop, 0)

        @pl.when(n > 0)
        def _():
            finish_sum(n - 1)

        return 0

    begin(jnp.int32(1))
    lax.fori_loop(0, n_z, root_mates, 0)
    lax.fori_loop(0, kids, kid, 0)
    last = jnp.int32(kids - 1)
    finish_sum(last)
    p_store(last).wait()
    t_store(last).wait()

    finish_line(0)

    def drain(n, _):
        finish_line(n + 1)
        for d in range(1, n_row):
            to_row(n, d).wait_send()

        def parts(at, _):
            @pl.when(at // per_row != r)
            def _():
                part_copy(n, at).wait_send()

            return 0

        lax.fori_loop(0, n_col, parts, 0)
        return 0

    lax.fori_loop(0, kids, drain, 0)


def body(n_row, n_col, root_inverse, factor, inverse_diag, structure):
    rows, kids, cols = factor.shape
    offset = lax.axis_index("row") * rows
    row_mask = jnp.repeat(structure, BLK, axis=1)
    local_mask = lax.dynamic_slice_in_dim(row_mask, offset, rows, 1).astype(factor.dtype)
    masked = jnp.transpose(factor, (1, 0, 2)) * local_mask[:, :, None]
    n_z = n_col // CORES
    per_row = rows // cols
    tile = min(256, rows)
    bf16 = jnp.bfloat16
    dma = pltpu.SemaphoreType.DMA
    flops = 4 * kids * rows * cols * rows * n_row
    block = jax.ShapeDtypeStruct((kids, rows, cols), bf16)
    p, total, _, _ = pl.pallas_call(
        functools.partial(kernel, n_row, n_col),
        out_shape=(
            block,
            block,
            jax.ShapeDtypeStruct((kids, n_col, rows, cols), bf16),
            jax.ShapeDtypeStruct((kids, n_row, rows, cols), bf16),
        ),
        in_specs=[pl.BlockSpec(memory_space=pl.ANY)] * 2,
        out_specs=(pl.BlockSpec(memory_space=pl.ANY),) * 4,
        scratch_shapes=[
            pltpu.VMEM((n_col, rows, cols), bf16),
            pltpu.VMEM((n_row, rows, cols), bf16),
            pltpu.VMEM((CORES, rows, cols), bf16),
            pltpu.VMEM((rows, cols), bf16),
            pltpu.VMEM((rows // tile, cols, tile), bf16),
            pltpu.VMEM((kids, n_col, cols, cols), bf16),
            pltpu.VMEM((kids, n_row, per_row, cols, cols), bf16),
            pltpu.VMEM((rows, cols), bf16),
            dma((3,)),
            dma((kids + 1, n_z - 1)),
            dma((kids + 1, n_z - 1)),
            dma((kids + 1, n_z - 1)),
            dma((kids + 1, n_z - 1)),
            dma((kids + 1, n_z)),
            dma((kids + 1, n_z)),
            dma((kids, n_row - 1)),
            dma((kids, n_row - 1)),
            dma((kids, n_col)),
            dma((kids, n_row, per_row)),
            dma((1 + CORES,)),
            dma(()),
            dma(()),
        ],
        compiler_params=pltpu.CompilerParams(
            collective_id=0, has_side_effects=True, vmem_limit_bytes=60 * 1024 * 1024),
        cost_estimate=pl.CostEstimate(
            flops=flops, bytes_accessed=64 * kids * rows * cols, transcendentals=0),
    )(root_inverse, masked)
    ainv_rk = jnp.transpose(p, (1, 0, 2))
    running = jnp.transpose(total, (1, 0, 2)).astype(jnp.float32)
    ainv_kk = (inverse_diag.astype(jnp.float32) - running).astype(bf16)
    return (ainv_rk, ainv_kk)


def solution(mesh):
    return jax.shard_map(
        functools.partial(body, mesh.shape["row"], mesh.shape["col"]),
        mesh=mesh,
        in_specs=(P("row", "col"), P("row", None, "col"), P("row", None, "col"), P()),
        out_specs=(P("row", None, "col"), P("row", None, "col")),
        check_vma=False,
    )
```

```python
import functools

import jax
import jax.numpy as jnp
from jax import lax
from jax.experimental import pallas as pl
from jax.experimental.pallas import tpu as pltpu
from jax.sharding import PartitionSpec as P

BLK = 128
CORES = 2
MESH = pl.DeviceIdType.MESH


def kernel(
    n_row, n_col, root_in, m_in, p_out, t_out, m_line, m_plane,
    root, col_buf, chunk_buf, p_buf, pt_buf, part_buf, sum_buf, t_buf,
    own_sem, up_send, up_recv, down_send, down_recv, mate_send, mate_recv,
    plane_send, plane_recv, part_send, part_recv, load_sem, out_sem, t_sem,
):
    kids, rows, cols = m_in.shape
    n_z = n_col // CORES
    per_row = rows // cols
    r, c = lax.axis_index("row"), lax.axis_index("col")
    z, core = c // CORES, c % CORES
    mate = z * CORES + 1 - core

    barrier = pltpu.get_barrier_semaphore()

    def greet(dev):
        pl.semaphore_signal(barrier, inc=1, device_id=dev, device_id_type=MESH)

    greet((r, mate))
    for d in range(1, n_row):
        greet((lax.rem(r + d, n_row), c))

    for step in (1, n_z - 1):
        greet((r, lax.rem(z + step, n_z) * CORES + core))

    own = [
        pltpu.make_async_copy(root_in, root.at[c], own_sem.at[0]),
        pltpu.make_async_copy(m_in, m_line.at[:, c], own_sem.at[1]),
        pltpu.make_async_copy(m_in, m_plane.at[:, r], own_sem.at[2]),
    ]
    for copy in own:
        copy.start()
    for copy in own:
        copy.wait()

    pl.semaphore_wait(barrier, n_row + 2)

    def slot(item, at):
        return root.at[at] if isinstance(item, int) else m_line.at[item - 1, at]

    def up(item, h, at):
        ref = slot(item, at)
        return pltpu.make_async_remote_copy(
            ref, ref, up_send.at[item, h], up_recv.at[item, h], (r, c + CORES), MESH)

    def down(item, h, at):
        ref = slot(item, at)
        return pltpu.make_async_remote_copy(
            ref, ref, down_send.at[item, h], down_recv.at[item, h], (r, c - CORES), MESH)

    def share(item, zz, at):
        ref = slot(item, at)
        return pltpu.make_async_remote_copy(
            ref, ref, mate_send.at[item, zz], mate_recv.at[item, zz], (r, mate), MESH)

    def begin(item):
        @pl.when(z < n_z - 1)
        def _():
            up(item, 0, c).start()

        @pl.when(z > 0)
        def _():
            down(item, 0, c).start()

        share(item, z, c).start()

    def arrive(item, h):
        low, high = z - 1 - h, z + 1 + h

        @pl.when(low >= 0)
        def _():
            at = low * CORES + core
            up(item, h, at).wait_recv()

            @pl.when((z < n_z - 1) & (h < n_z - 2))
            def _():
                up(item, h + 1, at).start()

            share(item, low, at).start()

        @pl.when(high < n_z)
        def _():
            at = high * CORES + core
            down(item, h, at).wait_recv()

            @pl.when((z > 0) & (h < n_z - 2))
            def _():
                down(item, h + 1, at).start()

            share(item, high, at).start()

    def finish_line(item):
        def hop(h, _):
            @pl.when((z < n_z - 1) & (z - h >= 0))
            def _():
                up(item, h, c - h * CORES).wait_send()

            @pl.when((z > 0) & (z + h < n_z))
            def _():
                down(item, h, c + h * CORES).wait_send()

            return 0

        lax.fori_loop(0, n_z - 1, hop, 0)

        def mates(zz, _):
            share(item, zz, zz * CORES + core).wait_send()
            return 0

        lax.fori_loop(0, n_z, mates, 0)

    def to_row(n, d):
        ref = m_plane.at[n, r]
        return pltpu.make_async_remote_copy(
            ref, ref, plane_send.at[n, d - 1], plane_recv.at[n, d - 1],
            (lax.rem(r + d, n_row), c), MESH)

    def from_row(n, d):
        ref = m_plane.at[n, lax.rem(r - d + n_row, n_row)]
        return pltpu.make_async_remote_copy(
            ref, ref, plane_send.at[n, d - 1], plane_recv.at[n, d - 1],
            (lax.rem(r + d, n_row), c), MESH)

    def send_plane(n):
        for d in range(1, n_row):
            to_row(n, d).start()

    def part_copy(n, at):
        half = lax.rem(at, per_row)
        return pltpu.make_async_remote_copy(
            part_buf.at[n, at], sum_buf.at[n, r, half], part_send.at[n, at],
            part_recv.at[n, r, half], (at // per_row, c), MESH)

    def p_store(n):
        return pltpu.make_async_copy(p_buf, p_out.at[n], out_sem)

    def make_p(n):
        for d in range(1, n_row):
            from_row(n, d).wait_recv()
        load = pltpu.make_async_copy(m_plane.at[n], col_buf, load_sem.at[0])
        load.start()

        @pl.when(n > 0)
        def _():
            p_store(n - 1).wait()

        load.wait()
        tile = min(256, rows)

        def one(t, _):
            at = pl.ds(pl.multiple_of(t * tile, tile), tile)
            total = jnp.zeros((tile, cols), jnp.float32)
            for k in range(n_col):
                block = col_buf[k // per_row, pl.ds((k % per_row) * cols, cols), :]
                total += jnp.dot(root[k, at, :], block, preferred_element_type=jnp.float32)
            total = -total
            p_buf[at, :] = total.astype(p_buf.dtype)
            pt_buf[t, :, :] = total.T.astype(pt_buf.dtype)
            return 0

        lax.fori_loop(0, rows // tile, one, 0)
        p_store(n).start()

    def consume(n, at):
        load = pltpu.make_async_copy(m_line.at[n, at], chunk_buf, load_sem.at[1])
        load.start()
        load.wait()
        tile = min(256, rows)
        part = jnp.zeros((cols, cols), jnp.float32)
        for t in range(rows // tile):
            part += jnp.dot(
                pt_buf[t, :, :], chunk_buf[pl.ds(t * tile, tile), :],
                preferred_element_type=jnp.float32)
        part = part.astype(part_buf.dtype)
        owner = at // per_row

        @pl.when(owner == r)
        def _():
            sum_buf[n, r, lax.rem(at, per_row)] = part

        @pl.when(owner != r)
        def _():
            part_buf[n, at] = part
            part_copy(n, at).start()

    def t_store(n):
        return pltpu.make_async_copy(t_buf, t_out.at[n], t_sem)

    def finish_sum(n):
        @pl.when(n > 0)
        def _():
            t_store(n - 1).wait()

        for half in range(per_row):
            total = jnp.zeros((cols, cols), jnp.float32)
            for d in range(1, n_row):
                src = lax.rem(r + d, n_row)
                ref = sum_buf.at[n, src, half]
                pltpu.make_async_remote_copy(
                    ref, ref, part_send.at[n, 0], part_recv.at[n, src, half],
                    (src, c), MESH).wait_recv()
            for src in range(n_row):
                total += sum_buf[n, src, half].astype(jnp.float32)
            t_buf[pl.ds(half * cols, cols), :] = total.T.astype(t_buf.dtype)
        t_store(n).start()

    def wait_mate(item, zz):
        share(item, zz, zz * CORES + 1 - core).wait_recv()

    def run_line(item):
        def hop(h, _):
            arrive(item, h)
            return 0

        lax.fori_loop(0, n_z - 1, hop, 0)

    def wait_mates(item):
        def one(zz, _):
            wait_mate(item, zz)
            return 0

        lax.fori_loop(0, n_z, one, 0)

    send_plane(0)
    begin(0)
    begin(jnp.int32(1))
    send_plane(1)
    run_line(0)
    begin(jnp.int32(2))
    wait_mates(0)
    for n in range(2, kids):
        send_plane(n)
    make_p(jnp.int32(0))
    run_line(jnp.int32(1))

    share_of = -(-n_col // (n_z - 1))

    def kid(n, _):
        @pl.when(n < kids - 2)
        def _():
            begin(n + 3)

        wait_mates(n + 1)

        def hop(h, _):
            def one(i, _):
                consume(n, lax.rem(i + (r + 1) * per_row, n_col))
                return 0

            lax.fori_loop(h * share_of, jnp.minimum((h + 1) * share_of, n_col), one, 0)

            @pl.when(n < kids - 1)
            def _():
                arrive(n + 2, h)

            return 0

        lax.fori_loop(0, n_z - 1, hop, 0)

        @pl.when(n < kids - 1)
        def _():
            make_p(n + 1)

        @pl.when(n > 0)
        def _():
            finish_sum(n - 1)

        return 0

    lax.fori_loop(0, kids, kid, 0)
    last = jnp.int32(kids - 1)
    finish_sum(last)
    p_store(last).wait()
    t_store(last).wait()

    finish_line(0)

    def drain(n, _):
        finish_line(n + 1)
        for d in range(1, n_row):
            to_row(n, d).wait_send()

        def parts(at, _):
            @pl.when(at // per_row != r)
            def _():
                part_copy(n, at).wait_send()

            return 0

        lax.fori_loop(0, n_col, parts, 0)
        return 0

    lax.fori_loop(0, kids, drain, 0)


def body(n_row, n_col, root_inverse, factor, inverse_diag, structure):
    rows, kids, cols = factor.shape
    offset = lax.axis_index("row") * rows
    row_mask = jnp.repeat(structure, BLK, axis=1)
    local_mask = lax.dynamic_slice_in_dim(row_mask, offset, rows, 1).astype(factor.dtype)
    masked = jnp.transpose(factor, (1, 0, 2)) * local_mask[:, :, None]
    n_z = n_col // CORES
    per_row = rows // cols
    tile = min(256, rows)
    bf16 = jnp.bfloat16
    dma = pltpu.SemaphoreType.DMA
    flops = 4 * kids * rows * cols * rows * n_row
    block = jax.ShapeDtypeStruct((kids, rows, cols), bf16)
    p, total, _, _ = pl.pallas_call(
        functools.partial(kernel, n_row, n_col),
        out_shape=(
            block,
            block,
            jax.ShapeDtypeStruct((kids, n_col, rows, cols), bf16),
            jax.ShapeDtypeStruct((kids, n_row, rows, cols), bf16),
        ),
        in_specs=[pl.BlockSpec(memory_space=pl.ANY)] * 2,
        out_specs=(pl.BlockSpec(memory_space=pl.ANY),) * 4,
        scratch_shapes=[
            pltpu.VMEM((n_col, rows, cols), bf16),
            pltpu.VMEM((n_row, rows, cols), bf16),
            pltpu.VMEM((rows, cols), bf16),
            pltpu.VMEM((rows, cols), bf16),
            pltpu.VMEM((rows // tile, cols, tile), bf16),
            pltpu.VMEM((kids, n_col, cols, cols), bf16),
            pltpu.VMEM((kids, n_row, per_row, cols, cols), bf16),
            pltpu.VMEM((rows, cols), bf16),
            dma((3,)),
            dma((kids + 1, n_z - 1)),
            dma((kids + 1, n_z - 1)),
            dma((kids + 1, n_z - 1)),
            dma((kids + 1, n_z - 1)),
            dma((kids + 1, n_z)),
            dma((kids + 1, n_z)),
            dma((kids, n_row - 1)),
            dma((kids, n_row - 1)),
            dma((kids, n_col)),
            dma((kids, n_row, per_row)),
            dma((2,)),
            dma(()),
            dma(()),
        ],
        compiler_params=pltpu.CompilerParams(
            collective_id=0, has_side_effects=True, vmem_limit_bytes=60 * 1024 * 1024),
        cost_estimate=pl.CostEstimate(
            flops=flops, bytes_accessed=64 * kids * rows * cols, transcendentals=0),
    )(root_inverse, masked)
    ainv_rk = jnp.transpose(p, (1, 0, 2))
    running = jnp.transpose(total, (1, 0, 2)).astype(jnp.float32)
    ainv_kk = (inverse_diag.astype(jnp.float32) - running).astype(bf16)
    return (ainv_rk, ainv_kk)


def solution(mesh):
    return jax.shard_map(
        functools.partial(body, mesh.shape["row"], mesh.shape["col"]),
        mesh=mesh,
        in_specs=(P("row", "col"), P("row", None, "col"), P("row", None, "col"), P()),
        out_specs=(P("row", None, "col"), P("row", None, "col")),
        check_vma=False,
    )
```

```python
import functools

import jax
import jax.numpy as jnp
from jax import lax
from jax.experimental import pallas as pl
from jax.experimental.pallas import tpu as pltpu
from jax.sharding import PartitionSpec as P

BLK = 128
CORES = 2
MESH = pl.DeviceIdType.MESH


def kernel(
    n_row, n_col, root_in, m_in, p_out, t_out, m_line, m_plane,
    root, col_buf, chunk_buf, p_buf, pt_buf, part_buf, sum_buf, t_buf,
    own_sem, up_send, up_recv, down_send, down_recv, mate_send, mate_recv,
    plane_send, plane_recv, part_send, part_recv, load_sem, out_sem, t_sem,
    flip_buf, flip_send, flip_recv,
):
    kids, rows, cols = m_in.shape
    n_z = n_col // CORES
    per_row = rows // cols
    r, c = lax.axis_index("row"), lax.axis_index("col")
    z, core = c // CORES, c % CORES
    mate = z * CORES + 1 - core

    def rises(item):
        return True if isinstance(item, int) else lax.rem(item, 2) == 1

    def sinks(item):
        return True if isinstance(item, int) else lax.rem(item, 2) == 0

    def held(item, zz):
        return (zz == z) | ((zz < z) & rises(item)) | ((zz > z) & sinks(item))

    barrier = pltpu.get_barrier_semaphore()

    def greet(dev):
        pl.semaphore_signal(barrier, inc=1, device_id=dev, device_id_type=MESH)

    greet((r, mate))
    for d in range(1, n_row):
        greet((lax.rem(r + d, n_row), c))

    for step in (1, n_z - 1):
        greet((r, lax.rem(z + step, n_z) * CORES + core))

    for half in range(per_row):
        greet((c // per_row, r * per_row + half))

    own = [
        pltpu.make_async_copy(root_in, root.at[c], own_sem.at[0]),
        pltpu.make_async_copy(m_in, m_line.at[:, c], own_sem.at[1]),
        pltpu.make_async_copy(m_in, m_plane.at[:, r], own_sem.at[2]),
    ]
    for copy in own:
        copy.start()
    for copy in own:
        copy.wait()

    pl.semaphore_wait(barrier, n_row + 2 + per_row)

    def slot(item, at):
        return root.at[at] if isinstance(item, int) else m_line.at[item - 1, at]

    def up(item, h, at):
        ref = slot(item, at)
        return pltpu.make_async_remote_copy(
            ref, ref, up_send.at[item, h], up_recv.at[item, h], (r, c + CORES), MESH)

    def down(item, h, at):
        ref = slot(item, at)
        return pltpu.make_async_remote_copy(
            ref, ref, down_send.at[item, h], down_recv.at[item, h], (r, c - CORES), MESH)

    def share(item, zz, at):
        ref = slot(item, at)
        return pltpu.make_async_remote_copy(
            ref, ref, mate_send.at[item, zz], mate_recv.at[item, zz], (r, mate), MESH)

    def begin(item):
        @pl.when((z < n_z - 1) & rises(item))
        def _():
            up(item, 0, c).start()

        @pl.when((z > 0) & sinks(item))
        def _():
            down(item, 0, c).start()

        share(item, z, c).start()

    def arrive(item, h):
        low, high = z - 1 - h, z + 1 + h

        @pl.when((low >= 0) & rises(item))
        def _():
            at = low * CORES + core
            up(item, h, at).wait_recv()

            @pl.when((z < n_z - 1) & (h < n_z - 2))
            def _():
                up(item, h + 1, at).start()

            share(item, low, at).start()

        @pl.when((high < n_z) & sinks(item))
        def _():
            at = high * CORES + core
            down(item, h, at).wait_recv()

            @pl.when((z > 0) & (h < n_z - 2))
            def _():
                down(item, h + 1, at).start()

            share(item, high, at).start()

    def finish_line(item):
        def hop(h, _):
            @pl.when((z < n_z - 1) & (z - h >= 0) & rises(item))
            def _():
                up(item, h, c - h * CORES).wait_send()

            @pl.when((z > 0) & (z + h < n_z) & sinks(item))
            def _():
                down(item, h, c + h * CORES).wait_send()

            return 0

        lax.fori_loop(0, n_z - 1, hop, 0)

        def mates(zz, _):
            @pl.when(held(item, zz))
            def _():
                share(item, zz, zz * CORES + core).wait_send()

            return 0

        lax.fori_loop(0, n_z, mates, 0)

    def to_row(n, d):
        ref = m_plane.at[n, r]
        return pltpu.make_async_remote_copy(
            ref, ref, plane_send.at[n, d - 1], plane_recv.at[n, d - 1],
            (lax.rem(r + d, n_row), c), MESH)

    def from_row(n, d):
        ref = m_plane.at[n, lax.rem(r - d + n_row, n_row)]
        return pltpu.make_async_remote_copy(
            ref, ref, plane_send.at[n, d - 1], plane_recv.at[n, d - 1],
            (lax.rem(r + d, n_row), c), MESH)

    def send_plane(n):
        for d in range(1, n_row):
            to_row(n, d).start()

    def part_copy(n, at):
        half = lax.rem(at, per_row)
        return pltpu.make_async_remote_copy(
            part_buf.at[n, at], sum_buf.at[n, r, half], part_send.at[n, at],
            part_recv.at[n, r, half], (at // per_row, c), MESH)

    def p_store(n):
        return pltpu.make_async_copy(p_buf, p_out.at[n], out_sem)

    def make_p(n):
        for d in range(1, n_row):
            from_row(n, d).wait_recv()
        load = pltpu.make_async_copy(m_plane.at[n], col_buf, load_sem.at[0])
        load.start()

        @pl.when(n > 0)
        def _():
            p_store(n - 1).wait()

        load.wait()
        tile = min(256, rows)

        def one(t, _):
            at = pl.ds(pl.multiple_of(t * tile, tile), tile)
            total = jnp.zeros((tile, cols), jnp.float32)
            for k in range(n_col):
                block = col_buf[k // per_row, pl.ds((k % per_row) * cols, cols), :]
                total += jnp.dot(root[k, at, :], block, preferred_element_type=jnp.float32)
            total = -total
            p_buf[at, :] = total.astype(p_buf.dtype)
            pt_buf[t, :, :] = total.T.astype(pt_buf.dtype)
            return 0

        lax.fori_loop(0, rows // tile, one, 0)
        p_store(n).start()

    def consume(n, at):
        load = pltpu.make_async_copy(m_line.at[n, at], chunk_buf, load_sem.at[1])
        load.start()
        load.wait()
        tile = min(256, rows)
        part = jnp.zeros((cols, cols), jnp.float32)
        for t in range(rows // tile):
            part += jnp.dot(
                pt_buf[t, :, :], chunk_buf[pl.ds(t * tile, tile), :],
                preferred_element_type=jnp.float32)
        part = part.astype(part_buf.dtype)
        owner = at // per_row

        @pl.when(owner == r)
        def _():
            sum_buf[n, r, lax.rem(at, per_row)] = part

        @pl.when(owner != r)
        def _():
            part_buf[n, at] = part
            part_copy(n, at).start()

    def t_store(n, half):
        at = pl.ds(half * cols, cols)
        return pltpu.make_async_copy(t_buf.at[n, at], t_out.at[n, at], t_sem.at[n, half])

    def flip(n, half):
        place = lax.rem(c, per_row)
        at = pl.ds(pl.multiple_of(place * cols, cols), cols)
        return pltpu.make_async_remote_copy(
            flip_buf.at[n, half], t_out.at[n, at], flip_send.at[n, half],
            flip_recv.at[n, place], (c // per_row, r * per_row + half), MESH)

    def flipped(n, half):
        return pltpu.make_async_remote_copy(
            flip_buf.at[n, half], t_out.at[n, pl.ds(half * cols, cols)],
            flip_send.at[n, half], flip_recv.at[n, half],
            (c // per_row, r * per_row + half), MESH)

    def finish_sum(n):
        for half in range(per_row):
            zz = (r * per_row + half) // CORES

            @pl.when(held(n + 1, zz))
            def _(half=half, zz=zz):
                total = jnp.zeros((cols, cols), jnp.float32)
                for d in range(1, n_row):
                    src = lax.rem(r + d, n_row)
                    ref = sum_buf.at[n, src, half]
                    pltpu.make_async_remote_copy(
                        ref, ref, part_send.at[n, 0], part_recv.at[n, src, half],
                        (src, c), MESH).wait_recv()
                for src in range(n_row):
                    total += sum_buf[n, src, half].astype(jnp.float32)

                @pl.when(zz != z)
                def _():
                    flip_buf[n, half] = total.astype(flip_buf.dtype)
                    flip(n, half).start()

                t_buf[n, pl.ds(half * cols, cols), :] = total.T.astype(t_buf.dtype)
                t_store(n, half).start()

    def finish_out(n):
        for half in range(per_row):
            zz = (r * per_row + half) // CORES

            @pl.when(held(n + 1, zz))
            def _(half=half, zz=zz):
                t_store(n, half).wait()

                @pl.when(zz != z)
                def _():
                    flip(n, half).wait_send()

            @pl.when(jnp.logical_not(held(n + 1, zz)))
            def _(half=half):
                flipped(n, half).wait_recv()

    def wait_mate(item, zz):
        share(item, zz, zz * CORES + 1 - core).wait_recv()

    def run_line(item):
        def hop(h, _):
            arrive(item, h)
            return 0

        lax.fori_loop(0, n_z - 1, hop, 0)

    def wait_mates(item):
        def one(zz, _):
            @pl.when(held(item, zz))
            def _():
                wait_mate(item, zz)

            return 0

        lax.fori_loop(0, n_z, one, 0)

    send_plane(0)
    begin(0)
    begin(jnp.int32(1))
    begin(jnp.int32(2))
    send_plane(1)
    run_line(0)
    for item in range(3, kids + 1):
        begin(jnp.int32(item))
    wait_mates(0)
    for n in range(2, kids):
        send_plane(n)
    make_p(jnp.int32(0))

    def first_hop(h, _):
        arrive(jnp.int32(1), h)
        arrive(jnp.int32(2), h)
        return 0

    lax.fori_loop(0, n_z - 1, first_hop, 0)

    share_of = -(-n_col // (n_z - 1))

    def kid(n, _):
        wait_mates(n + 1)

        def hop(h, _):
            def one(i, _):
                at = lax.rem(i + (r + 1) * per_row, n_col)

                @pl.when(held(n + 1, at // CORES))
                def _():
                    consume(n, at)

                return 0

            lax.fori_loop(h * share_of, jnp.minimum((h + 1) * share_of, n_col), one, 0)

            @pl.when((n < kids - 2) & (lax.rem(n, 2) == 0))
            def _():
                arrive(n + 3, h)
                arrive(n + 4, h)

            return 0

        lax.fori_loop(0, n_z - 1, hop, 0)

        @pl.when(n < kids - 1)
        def _():
            make_p(n + 1)

        @pl.when(n > 0)
        def _():
            finish_sum(n - 1)

        return 0

    lax.fori_loop(0, kids, kid, 0)
    last = jnp.int32(kids - 1)
    finish_sum(last)
    p_store(last).wait()

    finish_line(0)

    def drain(n, _):
        finish_line(n + 1)
        finish_out(n)
        for d in range(1, n_row):
            to_row(n, d).wait_send()

        def parts(at, _):
            @pl.when((at // per_row != r) & held(n + 1, at // CORES))
            def _():
                part_copy(n, at).wait_send()

            return 0

        lax.fori_loop(0, n_col, parts, 0)
        return 0

    lax.fori_loop(0, kids, drain, 0)


def body(n_row, n_col, root_inverse, factor, inverse_diag, structure):
    rows, kids, cols = factor.shape
    offset = lax.axis_index("row") * rows
    row_mask = jnp.repeat(structure, BLK, axis=1)
    local_mask = lax.dynamic_slice_in_dim(row_mask, offset, rows, 1).astype(factor.dtype)
    masked = jnp.transpose(factor, (1, 0, 2)) * local_mask[:, :, None]
    n_z = n_col // CORES
    per_row = rows // cols
    tile = min(256, rows)
    bf16 = jnp.bfloat16
    dma = pltpu.SemaphoreType.DMA
    flops = 4 * kids * rows * cols * rows * n_row
    block = jax.ShapeDtypeStruct((kids, rows, cols), bf16)
    p, total, _, _ = pl.pallas_call(
        functools.partial(kernel, n_row, n_col),
        out_shape=(
            block,
            block,
            jax.ShapeDtypeStruct((kids, n_col, rows, cols), bf16),
            jax.ShapeDtypeStruct((kids, n_row, rows, cols), bf16),
        ),
        in_specs=[pl.BlockSpec(memory_space=pl.ANY)] * 2,
        out_specs=(pl.BlockSpec(memory_space=pl.ANY),) * 4,
        scratch_shapes=[
            pltpu.VMEM((n_col, rows, cols), bf16),
            pltpu.VMEM((n_row, rows, cols), bf16),
            pltpu.VMEM((rows, cols), bf16),
            pltpu.VMEM((rows, cols), bf16),
            pltpu.VMEM((rows // tile, cols, tile), bf16),
            pltpu.VMEM((kids, n_col, cols, cols), bf16),
            pltpu.VMEM((kids, n_row, per_row, cols, cols), bf16),
            pltpu.VMEM((kids, rows, cols), bf16),
            dma((3,)),
            dma((kids + 1, n_z - 1)),
            dma((kids + 1, n_z - 1)),
            dma((kids + 1, n_z - 1)),
            dma((kids + 1, n_z - 1)),
            dma((kids + 1, n_z)),
            dma((kids + 1, n_z)),
            dma((kids, n_row - 1)),
            dma((kids, n_row - 1)),
            dma((kids, n_col)),
            dma((kids, n_row, per_row)),
            dma((2,)),
            dma(()),
            dma((kids, per_row)),
            pltpu.VMEM((kids, per_row, cols, cols), bf16),
            dma((kids, per_row)),
            dma((kids, per_row)),
        ],
        compiler_params=pltpu.CompilerParams(
            collective_id=0, has_side_effects=True, vmem_limit_bytes=60 * 1024 * 1024),
        cost_estimate=pl.CostEstimate(
            flops=flops, bytes_accessed=64 * kids * rows * cols, transcendentals=0),
    )(root_inverse, masked)
    ainv_rk = jnp.transpose(p, (1, 0, 2))
    running = jnp.transpose(total, (1, 0, 2)).astype(jnp.float32)
    ainv_kk = (inverse_diag.astype(jnp.float32) - running).astype(bf16)
    return (ainv_rk, ainv_kk)


def solution(mesh):
    return jax.shard_map(
        functools.partial(body, mesh.shape["row"], mesh.shape["col"]),
        mesh=mesh,
        in_specs=(P("row", "col"), P("row", None, "col"), P("row", None, "col"), P()),
        out_specs=(P("row", None, "col"), P("row", None, "col")),
        check_vma=False,
    )
```
